32 devices in a mesh: parts: 2 (over y), tensor: 4 (over z), dp: 4 (over x, core).
Axes of the slice: x: 2, y: 2, z: 4, core: 2. Of those that a mesh axis runs over, the one named last changes fastest.
Arguments:
- inputs: bfloat16 [3584, 8192], P(('parts', 'dp'), 'tensor'), parts along dimension 0, may hold values from -6 to 6
- out_grad: bfloat16 [3584, 8192], P(('parts', 'dp'), 'tensor'), parts along dimension 0, may hold values from -6 to 6
- gate_pre: bfloat16 [3584, 14784], P(('parts', 'dp'), 'tensor'), parts along dimension 0, may hold values from -5 to 5
- up_pre: bfloat16 [3584, 14784], P(('parts', 'dp'), 'tensor'), parts along dimension 0, may hold values from -5 to 5
- down_weight: bfloat16 [14784, 8192], P('tensor', 'dp'), may hold values from -0.0625 to 0.0625
- in_gate: bfloat16 [8192, 64], P('tensor'), may hold values from -0.0625 to 0.0625
- out_gate: bfloat16 [14784, 64], P('tensor'), may hold values from -0.046875 to 0.046875
- in_up: bfloat16 [8192, 64], P('tensor'), may hold values from -0.0625 to 0.0625
- out_up: bfloat16 [14784, 64], P('tensor'), may hold values from -0.046875 to 0.046875
- in_down: bfloat16 [14784, 64], P('tensor'), may hold values from -0.046875 to 0.046875
- out_down: bfloat16 [8192, 64], P('tensor'), may hold values from -0.0625 to 0.0625
- counts: int32 [16], P(('parts', 'dp')), parts along dimension 0, may hold values from 56 to 224, as said below
- query_ids: int32 [16], P('parts'), parts along dimension 0, may hold values from 0 to 7, as said below
Outputs:
- sketches: float32 [16, 3, 4096], P(('parts', 'dp')), parts along dimension 0
- scores: float32 [16, 8], P(('parts', 'dp')), parts along dimension 0
The draws below stay inside these ranges and needn't reach their ends.
There are 2 independent parts, one for each index of `parts`. The reference program is written for one: setup_inputs(seed, part) draws one part's arguments, and reference() takes and returns one part's arrays. A program takes and returns all parts, laid end to end along the dimension named above; an argument that names none is the same for every part. Nothing has to cross between parts.
Inputs may be any that keep to these rules, and one draw needn't show every extreme that they name: The valid tokens are the first counts[e] slots of example e. `query_ids`: distinct example indices.
All inputs are finite; a program needn't handle non-finite values.
Results may differ from the reference program's by a relative error of at most 0.0029.
Values may be sent and summed in bfloat16 or wider, within the bound.
A program may use at most 256 MiB of HBM per device.

```python
import math
import jax
import jax.numpy as jnp
from jax import lax

D = 8192
FF = 14784
RANK = 64
SEQ = 224
QUERIES = 8
EXAMPLES = 8
TOKENS = 1792


def draw_counts(key, part):
    key = jax.random.fold_in(key, 11)
    values = jax.random.randint(key, (EXAMPLES,), SEQ // 4, SEQ + 1).astype(jnp.int32)
    first = jax.random.randint(jax.random.fold_in(key, 1), (), 0, EXAMPLES).astype(jnp.int32)
    offset = jax.random.randint(jax.random.fold_in(key, 2), (), 0, EXAMPLES - 1).astype(jnp.int32)
    second = (first + 1 + offset) % EXAMPLES
    places = jnp.arange(EXAMPLES, dtype=jnp.int32)
    values = jnp.where(places == first, SEQ, values)
    values = jnp.where(places == second, SEQ // 4, values)
    return values.astype(jnp.int32)


def draw_query_ids(key, part):
    key = jax.random.fold_in(key, 23)
    middle = 1 + jax.random.permutation(key, EXAMPLES - 2)[:QUERIES - 2].astype(jnp.int32)
    chosen = jnp.concatenate([jnp.array([0, EXAMPLES - 1], dtype=jnp.int32), middle])
    order = jax.random.permutation(jax.random.fold_in(key, 3), QUERIES).astype(jnp.int32)
    return jnp.take(chosen, order).astype(jnp.int32)


def shard_levels(key, shape, pieces, smallest, high):
    loudness, own = 1.0, jax.random.fold_in(key, 6)
    for axis_at, blocks in pieces:
        draws = jnp.exp(jax.random.uniform(jax.random.fold_in(own, axis_at), (blocks,), jnp.float32, smallest / len(pieces), high / len(pieces)))
        loudness = loudness * jnp.repeat(draws, shape[axis_at] // blocks).reshape([-1 if axis == axis_at else 1 for axis in range(len(shape))])
    return loudness


def bell_draw(key, extent, deviation, limit, shards=(), kind=jnp.bfloat16):
    factor_of = shard_levels(key, extent, shards, -0.22, 0.18) if shards else 1.0
    values = jax.random.normal(key, extent, jnp.float32) * deviation * factor_of
    return jnp.minimum(jnp.maximum(values, -limit), limit).astype(kind)


def setup_inputs(seed: int = 0, part: int = 0) -> dict:
    streams_of = jax.random.split(jax.random.key(seed), 14)
    part_keys = jax.random.split(jax.random.fold_in(streams_of[13], part), 14)
    inputs = bell_draw(part_keys[0], (TOKENS, D), 1.0, 6.0, ((0, 4), (1, 4)))
    out_grad = bell_draw(part_keys[1], (TOKENS, D), 1.0, 6.0, ((0, 4), (1, 4)))
    gate_pre = bell_draw(part_keys[2], (TOKENS, FF), 1.0, 5.0, ((0, 4), (1, 4)))
    up_pre = bell_draw(part_keys[3], (TOKENS, FF), 1.0, 5.0, ((0, 4), (1, 4)))
    down_weight = bell_draw(streams_of[4], (FF, D), D ** -0.5, 0.0625, ((0, 4), (1, 4)))
    in_gate = bell_draw(streams_of[5], (D, RANK), D ** -0.5, 0.0625, ((0, 4),))
    out_gate = bell_draw(streams_of[6], (FF, RANK), FF ** -0.5, 0.046875, ((0, 4),))
    in_up = bell_draw(streams_of[7], (D, RANK), D ** -0.5, 0.0625, ((0, 4),))
    out_up = bell_draw(streams_of[8], (FF, RANK), FF ** -0.5, 0.046875, ((0, 4),))
    in_down = bell_draw(streams_of[9], (FF, RANK), FF ** -0.5, 0.046875, ((0, 4),))
    out_down = bell_draw(streams_of[10], (D, RANK), D ** -0.5, 0.0625, ((0, 4),))
    counts = draw_counts(jax.random.fold_in(jax.random.fold_in(streams_of[13], part), 71), part)
    query_ids = draw_query_ids(jax.random.fold_in(jax.random.fold_in(streams_of[13], part), 71), part)
    return {"inputs": inputs, "out_grad": out_grad, "gate_pre": gate_pre, "up_pre": up_pre, "down_weight": down_weight, "in_gate": in_gate, "out_gate": out_gate, "in_up": in_up, "out_up": out_up, "in_down": in_down, "out_down": out_down, "counts": counts, "query_ids": query_ids}


def token_weights(rows, counts):
    slot = rows // SEQ
    place = rows % SEQ
    owners = jnp.arange(counts.shape[0], dtype=jnp.int32)
    hit = (slot[None, :] == owners[:, None]) & (place[None, :] < counts[:, None])
    return hit.astype(jnp.float32) * (1.0 / math.sqrt(SEQ))

def outer_sums(proj, weights):
    shaped = proj.reshape(proj.shape[0], 3, 2, -1)
    result = jnp.einsum('en,nli,nlj->elij', weights, shaped[:, :, 0, :], shaped[:, :, 1, :], precision=lax.Precision.HIGHEST)
    return result.reshape(result.shape[0], 3, -1)

def cosines(sketches, query):
    left = sketches.reshape(sketches.shape[0], -1)
    right = query.reshape(query.shape[0], -1)
    inner = jnp.einsum('ef,qf->eq', left, right, precision=lax.Precision.HIGHEST)
    left_norm = jnp.sqrt(lax.optimization_barrier(jnp.sum(left * left, axis=1)) + 1e-06)
    right_norm = jnp.sqrt(lax.optimization_barrier(jnp.sum(right * right, axis=1)) + 1e-06)
    return inner / (left_norm[:, None] * right_norm[None, :])

def reference(inputs, out_grad, gate_pre, up_pre, down_weight, in_gate, out_gate, in_up, out_up, in_down, out_down, counts, query_ids):
    grad_hidden = jnp.dot(out_grad, down_weight.T, preferred_element_type=jnp.float32)
    gate_value = gate_pre.astype(jnp.float32)
    up_value = up_pre.astype(jnp.float32)
    sigmoid_gate = jax.nn.sigmoid(gate_value)
    hidden = (gate_value * sigmoid_gate * up_value).astype(jnp.bfloat16)
    grad_up = (grad_hidden * gate_value * sigmoid_gate).astype(jnp.bfloat16)
    grad_gate = (grad_hidden * up_value * sigmoid_gate * (1.0 + gate_value * (1.0 - sigmoid_gate))).astype(jnp.bfloat16)
    proj = jnp.concatenate([jnp.dot(inputs, in_gate, preferred_element_type=jnp.float32), jnp.dot(grad_gate, out_gate, preferred_element_type=jnp.float32), jnp.dot(inputs, in_up, preferred_element_type=jnp.float32), jnp.dot(grad_up, out_up, preferred_element_type=jnp.float32), jnp.dot(hidden, in_down, preferred_element_type=jnp.float32), jnp.dot(out_grad, out_down, preferred_element_type=jnp.float32)], axis=1)
    weights = token_weights(jnp.arange(proj.shape[0], dtype=jnp.int32), counts)
    sketches = outer_sums(proj, weights)
    query = jnp.take(sketches, query_ids, axis=0)
    return (sketches, cosines(sketches, query))
```

```python
import functools
import math

import jax
import jax.numpy as jnp
from jax import lax
from jax.experimental import pallas as pl
from jax.experimental.pallas import tpu as pltpu
from jax.sharding import PartitionSpec as P

SEQ = 224


def token_weights(rows, counts):
    slot = rows // SEQ
    place = rows % SEQ
    owners = jnp.arange(counts.shape[0], dtype=jnp.int32)
    hit = (slot[None, :] == owners[:, None]) & (place[None, :] < counts[:, None])
    return hit.astype(jnp.float32) * (1.0 / math.sqrt(SEQ))


def outer_sums(proj, weights):
    shaped = proj.reshape(proj.shape[0], 3, 2, -1)
    result = jnp.einsum(
        "en,nli,nlj->elij",
        weights,
        shaped[:, :, 0, :],
        shaped[:, :, 1, :],
        precision=lax.Precision.HIGHEST,
    )
    return result.reshape(result.shape[0], 3, -1)


def cosines(sketches, query):
    left = sketches.reshape(sketches.shape[0], -1)
    right = query.reshape(query.shape[0], -1)
    inner = jnp.einsum("ef,qf->eq", left, right, precision=lax.Precision.HIGHEST)
    left_norm = jnp.sqrt(jnp.sum(left * left, axis=1) + 1e-06)
    right_norm = jnp.sqrt(jnp.sum(right * right, axis=1) + 1e-06)
    return inner / (left_norm[:, None] * right_norm[None, :])


def contract_cols(left, right):
    return lax.dot_general(
        left, right, (((1,), (1,)), ((), ())), preferred_element_type=jnp.float32
    )


CHUNK = 256
AHEAD = 4
PIECES = 4
MESH = pl.DeviceIdType.MESH


def backprop_kernel(
    w_ref,
    g_ref,
    gate_ref,
    up_ref,
    og_ref,
    ou_ref,
    id_ref,
    proj_ref,
    wbuf,
    gbuf,
    gate_v,
    up_v,
    wv,
    own_sem,
    ld_sem,
    x_send,
    x_recv,
    y_send,
    y_recv,
    s_send,
    s_recv,
    dn_send,
    dn_recv,
    up_send,
    up_recv,
):
    hidden_rows, depth = w_ref.shape
    tokens = g_ref.shape[0]
    blocks = gbuf.shape[0]
    half = depth // 2
    full = hidden_rows // CHUNK
    last = hidden_rows - full * CHUNK
    piece = tokens // PIECES
    z_steps = PIECES * (blocks - 1)

    y = lax.axis_index("parts")
    z = lax.axis_index("tensor")
    d = lax.axis_index("dp")
    sib = d + 1 - 2 * (d % 2)
    far = (d + 2) % 4
    far_sib = far + 1 - 2 * (far % 2)

    def rows_of(k, rows):
        return pl.ds(pl.multiple_of(k * CHUNK, CHUNK), rows)

    def cols_of(h):
        return pl.ds(pl.multiple_of(h * half, half), half)

    def remote(src, dst, send, recv, device):
        return pltpu.make_async_remote_copy(
            src_ref=src,
            dst_ref=dst,
            send_sem=send,
            recv_sem=recv,
            device_id=device,
            device_id_type=MESH,
        )

    def x_copy(k, rows):
        r = rows_of(k, rows)
        return remote(
            w_ref.at[r, cols_of(y)],
            wbuf.at[d, r, cols_of(y)],
            x_send.at[k],
            x_recv.at[k],
            {"dp": far},
        )

    def x_arrival(k, rows):
        r = rows_of(k, rows)
        return remote(
            w_ref.at[r, cols_of(y)],
            wbuf.at[far, r, cols_of(y)],
            x_send.at[k],
            x_recv.at[k],
            {"dp": far},
        )

    def y_copy(k, rows):
        r = rows_of(k, rows)
        block = wbuf.at[far, r, cols_of(y)]
        return remote(block, block, y_send.at[k], y_recv.at[k], {"parts": 1 - y})

    def y_arrival(k, rows):
        r = rows_of(k, rows)
        block = wbuf.at[far, r, cols_of(1 - y)]
        return remote(block, block, y_send.at[k], y_recv.at[k], {"parts": 1 - y})

    def s0_copy(k, rows, block):
        r = rows_of(k, rows)
        return remote(
            w_ref.at[r], wbuf.at[block, r], s_send.at[0, k], s_recv.at[0, k], {"dp": sib}
        )

    def s_copy(kind, k, rows, block):
        r = rows_of(k, rows)
        h = y if kind == 1 else 1 - y
        view = wbuf.at[block, r, cols_of(h)]
        return remote(view, view, s_send.at[kind, k], s_recv.at[kind, k], {"dp": sib})

    def z_rows(n):
        return pl.ds(pl.multiple_of((n % PIECES) * piece, piece), piece)

    def dn_copy(n, first):
        view = gbuf.at[first + n // PIECES, z_rows(n)]
        return remote(view, view, dn_send.at[n], dn_recv.at[n], {"tensor": z - 1})

    def up_copy(n, first):
        view = gbuf.at[first - n // PIECES, z_rows(n)]
        return remote(view, view, up_send.at[n], up_recv.at[n], {"tensor": z + 1})

    def z_duty(n):
        @pl.when(n < PIECES * (blocks - 1 - z))
        def _():
            dn_copy(n, z + 1).wait_recv()

            @pl.when(z > 0)
            def _():
                dn_copy(n + PIECES, z).start()

        @pl.when(n < PIECES * z)
        def _():
            up_copy(n, z - 1).wait_recv()

            @pl.when(z < blocks - 1)
            def _():
                up_copy(n + PIECES, z).start()

    own_g = pltpu.make_async_copy(g_ref, gbuf.at[z], own_sem.at[0])
    own_w = pltpu.make_async_copy(w_ref, wbuf.at[d], own_sem.at[1])
    own_gate = pltpu.make_async_copy(gate_ref, gate_v, own_sem.at[2])
    own_up = pltpu.make_async_copy(up_ref, up_v, own_sem.at[3])
    own_g.start()

    barrier = pltpu.get_barrier_semaphore()
    for device in ({"dp": sib}, {"dp": far}, {"parts": 1 - y}):
        pl.semaphore_signal(barrier, inc=1, device_id=device, device_id_type=MESH)

    @pl.when(z > 0)
    def _():
        pl.semaphore_signal(barrier, inc=1, device_id={"tensor": z - 1}, device_id_type=MESH)

    @pl.when(z < blocks - 1)
    def _():
        pl.semaphore_signal(barrier, inc=1, device_id={"tensor": z + 1}, device_id_type=MESH)

    neighbours = 3 + (z > 0).astype(jnp.int32) + (z < blocks - 1).astype(jnp.int32)
    pl.semaphore_wait(barrier, neighbours)

    def open_chunk(k, rows):
        x_copy(k, rows).start()
        s0_copy(k, rows, d).start()

    for k in range(AHEAD):
        open_chunk(k, CHUNK)
    own_g.wait()

    @pl.when(z > 0)
    def _():
        for n in range(PIECES):
            dn_copy(n, z).start()

    @pl.when(z < blocks - 1)
    def _():
        for n in range(PIECES):
            up_copy(n, z).start()

    own_w.start()
    own_gate.start()
    own_up.start()
    proj_ref[...] = jnp.zeros_like(proj_ref)

    def take_x(k, rows):
        x_arrival(k, rows).wait_recv()
        y_copy(k, rows).start()
        s_copy(1, k, rows, far).start()
        s0_copy(k, rows, sib).wait_recv()

    def take_y(k, rows):
        y_arrival(k, rows).wait_recv()
        s_copy(2, k, rows, far).start()
        s_copy(1, k, rows, far_sib).wait_recv()

    def take_s(k, rows):
        s_copy(2, k, rows, far_sib).wait_recv()

    def traffic(k):
        take_x(k, CHUNK)

        @pl.when(k >= 1)
        def _():
            take_y(k - 1, CHUNK)

        @pl.when(k >= 2)
        def _():
            take_s(k - 2, CHUNK)

        @pl.when(k + AHEAD < full)
        def _():
            open_chunk(k + AHEAD, CHUNK)

        if last:

            @pl.when(k + AHEAD == full)
            def _():
                open_chunk(full, last)

    def loads(f, rows):
        slot = f % 2
        r = rows_of(f, rows)
        return [
            pltpu.make_async_copy(
                wbuf.at[b, r], wv.at[slot, b, pl.ds(0, rows)], ld_sem.at[slot, b]
            )
            for b in range(blocks)
        ]

    def tile(f, rows, next_rows):
        for copy in loads(f, rows):
            copy.wait()
        if next_rows:
            for copy in loads(f + 1, next_rows):
                copy.start()
        slot = f % 2
        r = rows_of(f, rows)
        grad = None
        for b in range(blocks):
            term = lax.dot_general(
                gbuf[b],
                wv[slot, b, pl.ds(0, rows), :],
                (((1,), (1,)), ((), ())),
                preferred_element_type=jnp.float32,
            )
            grad = term if grad is None else grad + term
        gate_value = gate_v[:, r].astype(jnp.float32)
        up_value = up_v[:, r].astype(jnp.float32)
        sig = 1.0 / (1.0 + jnp.exp(-gate_value))
        hidden = (gate_value * sig * up_value).astype(jnp.bfloat16)
        grad_up = (grad * gate_value * sig).astype(jnp.bfloat16)
        grad_gate = (grad * up_value * sig * (1.0 + gate_value * (1.0 - sig))).astype(jnp.bfloat16)
        proj_ref[0] += jnp.dot(grad_gate, og_ref[r, :], preferred_element_type=jnp.float32)
        proj_ref[1] += jnp.dot(grad_up, ou_ref[r, :], preferred_element_type=jnp.float32)
        proj_ref[2] += jnp.dot(hidden, id_ref[r, :], preferred_element_type=jnp.float32)

    def tiles(lo, hi):
        @pl.loop(lo, hi)
        def _(f):
            tile(f, CHUNK, CHUNK)

    @pl.loop(0, z_steps)
    def _(k):
        z_duty(k)
        traffic(k)

    own_w.wait()
    own_gate.wait()
    own_up.wait()
    for copy in loads(0, CHUNK):
        copy.start()

    done = 0
    for k in range(z_steps, full):
        traffic(k)
        ready = k - 2
        step = min(ready, done + 5)
        tiles(done, step)
        done = step
    if last:
        take_x(full, last)
    take_y(full - 1, CHUNK)
    take_s(full - 2, CHUNK)
    tiles(done, full - 2)
    if last:
        take_y(full, last)
    take_s(full - 1, CHUNK)
    tiles(full - 2, full - 1)
    if last:
        take_s(full, last)
    tile(full - 1, CHUNK, last)
    if last:
        tile(full, last, 0)

    def drain(k, rows):
        x_copy(k, rows).wait_send()
        y_copy(k, rows).wait_send()
        s0_copy(k, rows, d).wait_send()
        s_copy(1, k, rows, far).wait_send()
        s_copy(2, k, rows, far).wait_send()

    @pl.loop(0, full)
    def _(k):
        drain(k, CHUNK)

    if last:
        drain(full, last)

    @pl.loop(0, z_steps)
    def _(n):
        @pl.when((z > 0) & (n < PIECES * (blocks - z)))
        def _():
            dn_copy(n, z).wait_send()

        @pl.when((z < blocks - 1) & (n < PIECES * (z + 1)))
        def _():
            up_copy(n, z).wait_send()


def backprop(down_weight, out_grad, gate_pre, up_pre, out_gate, out_up, in_down, blocks):
    hidden_rows, depth = down_weight.shape
    tokens = out_grad.shape[0]
    rank = out_gate.shape[1]
    chunks = pl.cdiv(hidden_rows, CHUNK)
    z_steps = PIECES * (blocks - 1)
    anywhere = pl.BlockSpec(memory_space=pl.ANY)
    local = pl.BlockSpec(memory_space=pltpu.VMEM)
    dma = pltpu.SemaphoreType.DMA
    proj, _ = pl.pallas_call(
        backprop_kernel,
        out_shape=(
            jax.ShapeDtypeStruct((3, tokens, rank), jnp.float32),
            jax.ShapeDtypeStruct((blocks, hidden_rows, depth), jnp.bfloat16),
        ),
        in_specs=[anywhere] * 4 + [local] * 3,
        out_specs=(local, anywhere),
        scratch_shapes=[
            pltpu.VMEM((blocks, tokens, depth), jnp.bfloat16),
            pltpu.VMEM(gate_pre.shape, jnp.bfloat16),
            pltpu.VMEM(up_pre.shape, jnp.bfloat16),
            pltpu.VMEM((2, blocks, CHUNK, depth), jnp.bfloat16),
            dma((4,)),
            dma((2, blocks)),
            dma((chunks,)),
            dma((chunks,)),
            dma((chunks,)),
            dma((chunks,)),
            dma((3, chunks)),
            dma((3, chunks)),
            dma((z_steps,)),
            dma((z_steps,)),
            dma((z_steps,)),
            dma((z_steps,)),
        ],
        compiler_params=pltpu.CompilerParams(
            collective_id=0, has_side_effects=True, vmem_limit_bytes=50 * 2**20
        ),
        cost_estimate=pl.CostEstimate(
            flops=2 * tokens * hidden_rows * depth * blocks,
            bytes_accessed=2 * blocks * hidden_rows * depth * 2,
            transcendentals=tokens * hidden_rows,
        ),
    )(down_weight, out_grad, gate_pre, up_pre, out_gate, out_up, in_down)
    return proj


def gathered(out_grad, gate_pre, up_pre, down_weight, out_gate, out_up, in_down):
    full_grad = lax.all_gather(out_grad, "tensor", axis=1, tiled=True)
    grad_hidden = contract_cols(full_grad, lax.all_gather(down_weight, "dp", axis=1, tiled=True))
    gate_value = gate_pre.astype(jnp.float32)
    up_value = up_pre.astype(jnp.float32)
    sigmoid_gate = jax.nn.sigmoid(gate_value)
    hidden = (gate_value * sigmoid_gate * up_value).astype(jnp.bfloat16)
    grad_up = (grad_hidden * gate_value * sigmoid_gate).astype(jnp.bfloat16)
    grad_gate = (
        grad_hidden * up_value * sigmoid_gate * (1.0 + gate_value * (1.0 - sigmoid_gate))
    ).astype(jnp.bfloat16)
    return (
        jnp.dot(grad_gate, out_gate, preferred_element_type=jnp.float32),
        jnp.dot(grad_up, out_up, preferred_element_type=jnp.float32),
        jnp.dot(hidden, in_down, preferred_element_type=jnp.float32),
    )


def shards(
    fused,
    inputs,
    out_grad,
    gate_pre,
    up_pre,
    down_weight,
    in_gate,
    out_gate,
    in_up,
    out_up,
    in_down,
    out_down,
    counts,
    query_ids,
):
    tok_rows = inputs.shape[0]
    if fused:
        grads = backprop(
            down_weight, out_grad, gate_pre, up_pre, out_gate, out_up, in_down, lax.axis_size("tensor")
        )
    else:
        grads = gathered(out_grad, gate_pre, up_pre, down_weight, out_gate, out_up, in_down)
    partial_proj = jnp.concatenate(
        [
            jnp.dot(inputs, in_gate, preferred_element_type=jnp.float32),
            grads[0],
            jnp.dot(inputs, in_up, preferred_element_type=jnp.float32),
            grads[1],
            grads[2],
            jnp.dot(out_grad, out_down, preferred_element_type=jnp.float32),
        ],
        axis=1,
    )
    proj = lax.psum(partial_proj, "tensor")
    weights = token_weights(jnp.arange(tok_rows, dtype=jnp.int32), counts)
    sketches = outer_sums(proj, weights)
    every_sketch = lax.all_gather(sketches.astype(jnp.bfloat16), "dp", axis=0, tiled=True).astype(
        sketches.dtype
    )
    owners = jnp.arange(every_sketch.shape[0], dtype=jnp.int32)
    select = (query_ids[:, None] == owners[None, :]).astype(jnp.float32)
    query = jnp.einsum("qe,elf->qlf", select, every_sketch, precision=lax.Precision.HIGHEST)
    return (sketches, cosines(sketches, query))


def solution(mesh):
    sizes = dict(mesh.shape)
    fused = sizes["parts"] == 2 and sizes["dp"] == 4 and sizes["tensor"] == 4
    return jax.shard_map(
        functools.partial(shards, fused),
        mesh=mesh,
        in_specs=(
            P(("parts", "dp"), "tensor"),
            P(("parts", "dp"), "tensor"),
            P(("parts", "dp"), "tensor"),
            P(("parts", "dp"), "tensor"),
            P("tensor", "dp"),
            P("tensor", None),
            P("tensor", None),
            P("tensor", None),
            P("tensor", None),
            P("tensor", None),
            P("tensor", None),
            P(("parts", "dp")),
            P("parts"),
        ),
        out_specs=(P(("parts", "dp"), None, None), P(("parts", "dp"), None)),
        check_vma=False,
    )
```

```python
import functools
import math

import jax
import jax.numpy as jnp
from jax import lax
from jax.experimental import pallas as pl
from jax.experimental.pallas import tpu as pltpu
from jax.sharding import PartitionSpec as P

SEQ = 224


def token_weights(rows, counts):
    slot = rows // SEQ
    place = rows % SEQ
    owners = jnp.arange(counts.shape[0], dtype=jnp.int32)
    hit = (slot[None, :] == owners[:, None]) & (place[None, :] < counts[:, None])
    return hit.astype(jnp.float32) * (1.0 / math.sqrt(SEQ))


def outer_sums(proj, weights):
    shaped = proj.reshape(proj.shape[0], 3, 2, -1)
    result = jnp.einsum(
        "en,nli,nlj->elij",
        weights,
        shaped[:, :, 0, :],
        shaped[:, :, 1, :],
        precision=lax.Precision.HIGHEST,
    )
    return result.reshape(result.shape[0], 3, -1)


def cosines(sketches, query):
    left = sketches.reshape(sketches.shape[0], -1)
    right = query.reshape(query.shape[0], -1)
    inner = jnp.einsum("ef,qf->eq", left, right, precision=lax.Precision.HIGHEST)
    left_norm = jnp.sqrt(jnp.sum(left * left, axis=1) + 1e-06)
    right_norm = jnp.sqrt(jnp.sum(right * right, axis=1) + 1e-06)
    return inner / (left_norm[:, None] * right_norm[None, :])


def contract_cols(left, right):
    return lax.dot_general(
        left, right, (((1,), (1,)), ((), ())), preferred_element_type=jnp.float32
    )


CHUNK = 256
AHEAD = 4
PIECES = 4
MESH = pl.DeviceIdType.MESH


def backprop_kernel(
    w_ref,
    g_ref,
    gate_ref,
    up_ref,
    og_ref,
    ou_ref,
    id_ref,
    proj_ref,
    wbuf,
    gbuf,
    gate_v,
    up_v,
    wv,
    own_sem,
    ld_sem,
    x_send,
    x_recv,
    y_send,
    y_recv,
    s_send,
    s_recv,
    dn_send,
    dn_recv,
    up_send,
    up_recv,
):
    hidden_rows, depth = w_ref.shape
    tokens = g_ref.shape[0]
    blocks = gbuf.shape[0]
    half = depth // 2
    full = hidden_rows // CHUNK
    last = hidden_rows - full * CHUNK
    piece = tokens // PIECES
    z_steps = PIECES * (blocks - 1)

    y = lax.axis_index("parts")
    z = lax.axis_index("tensor")
    d = lax.axis_index("dp")
    sib = d + 1 - 2 * (d % 2)
    far = (d + 2) % 4
    far_sib = far + 1 - 2 * (far % 2)
    order = (d, sib, far, far_sib)

    def rows_of(k, rows):
        return pl.ds(pl.multiple_of(k * CHUNK, CHUNK), rows)

    def cols_of(h):
        return pl.ds(pl.multiple_of(h * half, half), half)

    def remote(src, dst, send, recv, device):
        return pltpu.make_async_remote_copy(
            src_ref=src,
            dst_ref=dst,
            send_sem=send,
            recv_sem=recv,
            device_id=device,
            device_id_type=MESH,
        )

    def x_copy(k, rows):
        r = rows_of(k, rows)
        return remote(
            w_ref.at[r, cols_of(y)],
            wbuf.at[d, r, cols_of(y)],
            x_send.at[k],
            x_recv.at[k],
            {"dp": far},
        )

    def x_arrival(k, rows):
        r = rows_of(k, rows)
        return remote(
            w_ref.at[r, cols_of(y)],
            wbuf.at[far, r, cols_of(y)],
            x_send.at[k],
            x_recv.at[k],
            {"dp": far},
        )

    def y_copy(k, rows):
        r = rows_of(k, rows)
        block = wbuf.at[far, r, cols_of(y)]
        return remote(block, block, y_send.at[k], y_recv.at[k], {"parts": 1 - y})

    def y_arrival(k, rows):
        r = rows_of(k, rows)
        block = wbuf.at[far, r, cols_of(1 - y)]
        return remote(block, block, y_send.at[k], y_recv.at[k], {"parts": 1 - y})

    def s0_copy(k, rows, block):
        r = rows_of(k, rows)
        return remote(
            w_ref.at[r], wbuf.at[block, r], s_send.at[0, k], s_recv.at[0, k], {"dp": sib}
        )

    def s_copy(kind, k, rows, block):
        r = rows_of(k, rows)
        h = y if kind == 1 else 1 - y
        view = wbuf.at[block, r, cols_of(h)]
        return remote(view, view, s_send.at[kind, k], s_recv.at[kind, k], {"dp": sib})

    def z_rows(n):
        return pl.ds(pl.multiple_of((n % PIECES) * piece, piece), piece)

    def dn_copy(n, first):
        view = gbuf.at[first + n // PIECES, z_rows(n)]
        return remote(view, view, dn_send.at[n], dn_recv.at[n], {"tensor": z - 1})

    def up_copy(n, first):
        view = gbuf.at[first - n // PIECES, z_rows(n)]
        return remote(view, view, up_send.at[n], up_recv.at[n], {"tensor": z + 1})

    def z_duty(n):
        @pl.when(n < PIECES * (blocks - 1 - z))
        def _():
            dn_copy(n, z + 1).wait_recv()

            @pl.when(z > 0)
            def _():
                dn_copy(n + PIECES, z).start()

        @pl.when(n < PIECES * z)
        def _():
            up_copy(n, z - 1).wait_recv()

            @pl.when(z < blocks - 1)
            def _():
                up_copy(n + PIECES, z).start()

    own_g = pltpu.make_async_copy(g_ref, gbuf.at[z], own_sem.at[0])
    own_gate = pltpu.make_async_copy(gate_ref, gate_v, own_sem.at[1])
    own_up = pltpu.make_async_copy(up_ref, up_v, own_sem.at[2])
    own_g.start()

    barrier = pltpu.get_barrier_semaphore()
    for device in ({"dp": sib}, {"dp": far}, {"parts": 1 - y}):
        pl.semaphore_signal(barrier, inc=1, device_id=device, device_id_type=MESH)

    @pl.when(z > 0)
    def _():
        pl.semaphore_signal(barrier, inc=1, device_id={"tensor": z - 1}, device_id_type=MESH)

    @pl.when(z < blocks - 1)
    def _():
        pl.semaphore_signal(barrier, inc=1, device_id={"tensor": z + 1}, device_id_type=MESH)

    neighbours = 3 + (z > 0).astype(jnp.int32) + (z < blocks - 1).astype(jnp.int32)
    pl.semaphore_wait(barrier, neighbours)

    def open_chunk(k, rows):
        x_copy(k, rows).start()
        s0_copy(k, rows, d).start()

    for k in range(AHEAD):
        open_chunk(k, CHUNK)
    own_g.wait()

    @pl.when(z > 0)
    def _():
        for n in range(PIECES):
            dn_copy(n, z).start()

    @pl.when(z < blocks - 1)
    def _():
        for n in range(PIECES):
            up_copy(n, z).start()

    own_gate.start()
    own_up.start()
    proj_ref[...] = jnp.zeros_like(proj_ref)

    def take_x(k, rows):
        x_arrival(k, rows).wait_recv()
        y_copy(k, rows).start()
        s_copy(1, k, rows, far).start()
        s0_copy(k, rows, sib).wait_recv()

    def take_y(k, rows):
        y_arrival(k, rows).wait_recv()
        s_copy(2, k, rows, far).start()
        s_copy(1, k, rows, far_sib).wait_recv()

    def take_s(k, rows):
        s_copy(2, k, rows, far_sib).wait_recv()

    def traffic(k):
        take_x(k, CHUNK)

        @pl.when(k >= 1)
        def _():
            take_y(k - 1, CHUNK)

        @pl.when(k >= 2)
        def _():
            take_s(k - 2, CHUNK)

        @pl.when(k + AHEAD < full)
        def _():
            open_chunk(k + AHEAD, CHUNK)

        if last:

            @pl.when(k + AHEAD == full)
            def _():
                open_chunk(full, last)

    def loads(f, rows):
        slot = f % 2
        r = rows_of(f, rows)
        sources = [w_ref.at[r]] + [wbuf.at[b, r] for b in order[1:]]
        return [
            pltpu.make_async_copy(src, wv.at[slot, j, pl.ds(0, rows)], ld_sem.at[slot, j])
            for j, src in enumerate(sources)
        ]

    def tile(f, rows, next_rows):
        for copy in loads(f, rows):
            copy.wait()
        if next_rows:
            for copy in loads(f + 1, next_rows):
                copy.start()
        slot = f % 2
        r = rows_of(f, rows)
        grad = None
        for j, b in enumerate(order):
            term = lax.dot_general(
                gbuf[b],
                wv[slot, j, pl.ds(0, rows), :],
                (((1,), (1,)), ((), ())),
                preferred_element_type=jnp.float32,
            )
            grad = term if grad is None else grad + term
        gate_value = gate_v[:, r].astype(jnp.float32)
        up_value = up_v[:, r].astype(jnp.float32)
        sig = 1.0 / (1.0 + jnp.exp(-gate_value))
        hidden = (gate_value * sig * up_value).astype(jnp.bfloat16)
        grad_up = (grad * gate_value * sig).astype(jnp.bfloat16)
        grad_gate = (grad * up_value * sig * (1.0 + gate_value * (1.0 - sig))).astype(jnp.bfloat16)
        proj_ref[0] += jnp.dot(grad_gate, og_ref[r, :], preferred_element_type=jnp.float32)
        proj_ref[1] += jnp.dot(grad_up, ou_ref[r, :], preferred_element_type=jnp.float32)
        proj_ref[2] += jnp.dot(hidden, id_ref[r, :], preferred_element_type=jnp.float32)

    def tiles(lo, hi):
        @pl.loop(lo, hi)
        def _(f):
            tile(f, CHUNK, CHUNK)

    @pl.loop(0, z_steps)
    def _(k):
        z_duty(k)
        traffic(k)

    own_gate.wait()
    own_up.wait()
    for copy in loads(0, CHUNK):
        copy.start()

    done = 0
    for k in range(z_steps, full):
        traffic(k)
        ready = k - 2
        step = min(ready, done + 5)
        tiles(done, step)
        done = step
    if last:
        take_x(full, last)
    take_y(full - 1, CHUNK)
    take_s(full - 2, CHUNK)
    tiles(done, full - 2)
    if last:
        take_y(full, last)
    take_s(full - 1, CHUNK)
    tiles(full - 2, full - 1)
    if last:
        take_s(full, last)
    tile(full - 1, CHUNK, last)
    if last:
        tile(full, last, 0)

    def drain(k, rows):
        x_copy(k, rows).wait_send()
        y_copy(k, rows).wait_send()
        s0_copy(k, rows, d).wait_send()
        s_copy(1, k, rows, far).wait_send()
        s_copy(2, k, rows, far).wait_send()

    @pl.loop(0, full)
    def _(k):
        drain(k, CHUNK)

    if last:
        drain(full, last)

    @pl.loop(0, z_steps)
    def _(n):
        @pl.when((z > 0) & (n < PIECES * (blocks - z)))
        def _():
            dn_copy(n, z).wait_send()

        @pl.when((z < blocks - 1) & (n < PIECES * (z + 1)))
        def _():
            up_copy(n, z).wait_send()


def backprop(down_weight, out_grad, gate_pre, up_pre, out_gate, out_up, in_down, blocks):
    hidden_rows, depth = down_weight.shape
    tokens = out_grad.shape[0]
    rank = out_gate.shape[1]
    chunks = pl.cdiv(hidden_rows, CHUNK)
    z_steps = PIECES * (blocks - 1)
    anywhere = pl.BlockSpec(memory_space=pl.ANY)
    local = pl.BlockSpec(memory_space=pltpu.VMEM)
    dma = pltpu.SemaphoreType.DMA
    proj, _ = pl.pallas_call(
        backprop_kernel,
        out_shape=(
            jax.ShapeDtypeStruct((3, tokens, rank), jnp.float32),
            jax.ShapeDtypeStruct((blocks, hidden_rows, depth), jnp.bfloat16),
        ),
        in_specs=[anywhere] * 4 + [local] * 3,
        out_specs=(local, anywhere),
        scratch_shapes=[
            pltpu.VMEM((blocks, tokens, depth), jnp.bfloat16),
            pltpu.VMEM(gate_pre.shape, jnp.bfloat16),
            pltpu.VMEM(up_pre.shape, jnp.bfloat16),
            pltpu.VMEM((2, blocks, CHUNK, depth), jnp.bfloat16),
            dma((3,)),
            dma((2, blocks)),
            dma((chunks,)),
            dma((chunks,)),
            dma((chunks,)),
            dma((chunks,)),
            dma((3, chunks)),
            dma((3, chunks)),
            dma((z_steps,)),
            dma((z_steps,)),
            dma((z_steps,)),
            dma((z_steps,)),
        ],
        compiler_params=pltpu.CompilerParams(
            collective_id=0, has_side_effects=True, vmem_limit_bytes=50 * 2**20
        ),
        cost_estimate=pl.CostEstimate(
            flops=2 * tokens * hidden_rows * depth * blocks,
            bytes_accessed=2 * blocks * hidden_rows * depth * 2,
            transcendentals=tokens * hidden_rows,
        ),
    )(down_weight, out_grad, gate_pre, up_pre, out_gate, out_up, in_down)
    return proj


def gathered(out_grad, gate_pre, up_pre, down_weight, out_gate, out_up, in_down):
    full_grad = lax.all_gather(out_grad, "tensor", axis=1, tiled=True)
    grad_hidden = contract_cols(full_grad, lax.all_gather(down_weight, "dp", axis=1, tiled=True))
    gate_value = gate_pre.astype(jnp.float32)
    up_value = up_pre.astype(jnp.float32)
    sigmoid_gate = jax.nn.sigmoid(gate_value)
    hidden = (gate_value * sigmoid_gate * up_value).astype(jnp.bfloat16)
    grad_up = (grad_hidden * gate_value * sigmoid_gate).astype(jnp.bfloat16)
    grad_gate = (
        grad_hidden * up_value * sigmoid_gate * (1.0 + gate_value * (1.0 - sigmoid_gate))
    ).astype(jnp.bfloat16)
    return (
        jnp.dot(grad_gate, out_gate, preferred_element_type=jnp.float32),
        jnp.dot(grad_up, out_up, preferred_element_type=jnp.float32),
        jnp.dot(hidden, in_down, preferred_element_type=jnp.float32),
    )


def shards(
    fused,
    inputs,
    out_grad,
    gate_pre,
    up_pre,
    down_weight,
    in_gate,
    out_gate,
    in_up,
    out_up,
    in_down,
    out_down,
    counts,
    query_ids,
):
    tok_rows = inputs.shape[0]
    if fused:
        grads = backprop(
            down_weight, out_grad, gate_pre, up_pre, out_gate, out_up, in_down, lax.axis_size("tensor")
        )
    else:
        grads = gathered(out_grad, gate_pre, up_pre, down_weight, out_gate, out_up, in_down)
    partial_proj = jnp.concatenate(
        [
            jnp.dot(inputs, in_gate, preferred_element_type=jnp.float32),
            grads[0],
            jnp.dot(inputs, in_up, preferred_element_type=jnp.float32),
            grads[1],
            grads[2],
            jnp.dot(out_grad, out_down, preferred_element_type=jnp.float32),
        ],
        axis=1,
    )
    proj = lax.psum(partial_proj, "tensor")
    weights = token_weights(jnp.arange(tok_rows, dtype=jnp.int32), counts)
    sketches = outer_sums(proj, weights)
    every_sketch = lax.all_gather(sketches.astype(jnp.bfloat16), "dp", axis=0, tiled=True).astype(
        sketches.dtype
    )
    owners = jnp.arange(every_sketch.shape[0], dtype=jnp.int32)
    select = (query_ids[:, None] == owners[None, :]).astype(jnp.float32)
    query = jnp.einsum("qe,elf->qlf", select, every_sketch, precision=lax.Precision.HIGHEST)
    return (sketches, cosines(sketches, query))


def solution(mesh):
    sizes = dict(mesh.shape)
    fused = sizes["parts"] == 2 and sizes["dp"] == 4 and sizes["tensor"] == 4
    return jax.shard_map(
        functools.partial(shards, fused),
        mesh=mesh,
        in_specs=(
            P(("parts", "dp"), "tensor"),
            P(("parts", "dp"), "tensor"),
            P(("parts", "dp"), "tensor"),
            P(("parts", "dp"), "tensor"),
            P("tensor", "dp"),
            P("tensor", None),
            P("tensor", None),
            P("tensor", None),
            P("tensor", None),
            P("tensor", None),
            P("tensor", None),
            P(("parts", "dp")),
            P("parts"),
        ),
        out_specs=(P(("parts", "dp"), None, None), P(("parts", "dp"), None)),
        check_vma=False,
    )
```

```python
import functools
import math

import jax
import jax.numpy as jnp
from jax import lax
from jax.experimental import pallas as pl
from jax.experimental.pallas import tpu as pltpu
from jax.sharding import PartitionSpec as P

SEQ = 224


def token_weights(rows, counts):
    slot = rows // SEQ
    place = rows % SEQ
    owners = jnp.arange(counts.shape[0], dtype=jnp.int32)
    hit = (slot[None, :] == owners[:, None]) & (place[None, :] < counts[:, None])
    return hit.astype(jnp.float32) * (1.0 / math.sqrt(SEQ))


def outer_sums(proj, weights):
    shaped = proj.reshape(proj.shape[0], 3, 2, -1)
    result = jnp.einsum(
        "en,nli,nlj->elij",
        weights,
        shaped[:, :, 0, :],
        shaped[:, :, 1, :],
        precision=lax.Precision.HIGHEST,
    )
    return result.reshape(result.shape[0], 3, -1)


def cosines(sketches, query):
    left = sketches.reshape(sketches.shape[0], -1)
    right = query.reshape(query.shape[0], -1)
    inner = jnp.einsum("ef,qf->eq", left, right, precision=lax.Precision.HIGHEST)
    left_norm = jnp.sqrt(jnp.sum(left * left, axis=1) + 1e-06)
    right_norm = jnp.sqrt(jnp.sum(right * right, axis=1) + 1e-06)
    return inner / (left_norm[:, None] * right_norm[None, :])


def contract_cols(left, right):
    return lax.dot_general(
        left, right, (((1,), (1,)), ((), ())), preferred_element_type=jnp.float32
    )


CHUNK = 256
AHEAD = 4
PIECES = 4
MESH = pl.DeviceIdType.MESH


def backprop_kernel(
    w_ref,
    g_ref,
    gate_ref,
    up_ref,
    og_ref,
    ou_ref,
    id_ref,
    proj_ref,
    wbuf,
    gbuf,
    gate_v,
    up_v,
    wv,
    own_sem,
    ld_sem,
    x_send,
    x_recv,
    y_send,
    y_recv,
    s_send,
    s_recv,
    dn_send,
    dn_recv,
    up_send,
    up_recv,
):
    hidden_rows, depth = w_ref.shape
    tokens = g_ref.shape[0]
    blocks = gbuf.shape[0]
    half = depth // 2
    full = hidden_rows // CHUNK
    last = hidden_rows - full * CHUNK
    piece = tokens // PIECES
    z_steps = PIECES * (blocks - 1)

    y = lax.axis_index("parts")
    z = lax.axis_index("tensor")
    d = lax.axis_index("dp")
    sib = d + 1 - 2 * (d % 2)
    far = (d + 2) % 4
    far_sib = far + 1 - 2 * (far % 2)
    order = (d, sib, far, far_sib)

    def rows_of(k, rows):
        return pl.ds(pl.multiple_of(k * CHUNK, CHUNK), rows)

    def cols_of(h):
        return pl.ds(pl.multiple_of(h * half, half), half)

    def remote(src, dst, send, recv, device):
        return pltpu.make_async_remote_copy(
            src_ref=src,
            dst_ref=dst,
            send_sem=send,
            recv_sem=recv,
            device_id=device,
            device_id_type=MESH,
        )

    def x_copy(k, rows):
        r = rows_of(k, rows)
        return remote(
            w_ref.at[r, cols_of(y)],
            wbuf.at[d, r, cols_of(y)],
            x_send.at[k],
            x_recv.at[k],
            {"dp": far},
        )

    def x_arrival(k, rows):
        r = rows_of(k, rows)
        return remote(
            w_ref.at[r, cols_of(y)],
            wbuf.at[far, r, cols_of(y)],
            x_send.at[k],
            x_recv.at[k],
            {"dp": far},
        )

    def y_copy(k, rows):
        r = rows_of(k, rows)
        block = wbuf.at[far, r, cols_of(y)]
        return remote(block, block, y_send.at[k], y_recv.at[k], {"parts": 1 - y})

    def y_arrival(k, rows):
        r = rows_of(k, rows)
        block = wbuf.at[far, r, cols_of(1 - y)]
        return remote(block, block, y_send.at[k], y_recv.at[k], {"parts": 1 - y})

    def s0_copy(k, rows, block):
        r = rows_of(k, rows)
        return remote(
            w_ref.at[r], wbuf.at[block, r], s_send.at[0, k], s_recv.at[0, k], {"dp": sib}
        )

    def s_copy(kind, k, rows, block):
        r = rows_of(k, rows)
        h = y if kind == 1 else 1 - y
        view = wbuf.at[block, r, cols_of(h)]
        return remote(view, view, s_send.at[kind, k], s_recv.at[kind, k], {"dp": sib})

    def z_rows(n):
        return pl.ds(pl.multiple_of((n % PIECES) * piece, piece), piece)

    def dn_copy(n, first):
        view = gbuf.at[first + n // PIECES, z_rows(n)]
        return remote(view, view, dn_send.at[n], dn_recv.at[n], {"tensor": z - 1})

    def up_copy(n, first):
        view = gbuf.at[first - n // PIECES, z_rows(n)]
        return remote(view, view, up_send.at[n], up_recv.at[n], {"tensor": z + 1})

    def z_duty(n):
        @pl.when(n < PIECES * (blocks - 1 - z))
        def _():
            dn_copy(n, z + 1).wait_recv()

            @pl.when(z > 0)
            def _():
                dn_copy(n + PIECES, z).start()

        @pl.when(n < PIECES * z)
        def _():
            up_copy(n, z - 1).wait_recv()

            @pl.when(z < blocks - 1)
            def _():
                up_copy(n + PIECES, z).start()

    own_g = pltpu.make_async_copy(g_ref, gbuf.at[z], own_sem.at[0])
    own_gate = pltpu.make_async_copy(gate_ref, gate_v, own_sem.at[1])
    own_up = pltpu.make_async_copy(up_ref, up_v, own_sem.at[2])
    own_g.start()

    barrier = pltpu.get_barrier_semaphore()
    for device in ({"dp": sib}, {"dp": far}, {"parts": 1 - y}):
        pl.semaphore_signal(barrier, inc=1, device_id=device, device_id_type=MESH)

    @pl.when(z > 0)
    def _():
        pl.semaphore_signal(barrier, inc=1, device_id={"tensor": z - 1}, device_id_type=MESH)

    @pl.when(z < blocks - 1)
    def _():
        pl.semaphore_signal(barrier, inc=1, device_id={"tensor": z + 1}, device_id_type=MESH)

    neighbours = 3 + (z > 0).astype(jnp.int32) + (z < blocks - 1).astype(jnp.int32)
    pl.semaphore_wait(barrier, neighbours)

    def open_chunk(k, rows):
        x_copy(k, rows).start()
        s0_copy(k, rows, d).start()

    for k in range(AHEAD):
        open_chunk(k, CHUNK)
    own_g.wait()

    @pl.when(z > 0)
    def _():
        for n in range(PIECES):
            dn_copy(n, z).start()

    @pl.when(z < blocks - 1)
    def _():
        for n in range(PIECES):
            up_copy(n, z).start()

    own_gate.start()
    own_up.start()
    proj_ref[...] = jnp.zeros_like(proj_ref)

    def take_x(k, rows):
        x_arrival(k, rows).wait_recv()
        y_copy(k, rows).start()
        s_copy(1, k, rows, far).start()
        s0_copy(k, rows, sib).wait_recv()

    def take_y(k, rows):
        y_arrival(k, rows).wait_recv()
        s_copy(2, k, rows, far).start()
        s_copy(1, k, rows, far_sib).wait_recv()

    def take_s(k, rows):
        s_copy(2, k, rows, far_sib).wait_recv()

    def traffic(k):
        take_x(k, CHUNK)

        @pl.when(k >= 1)
        def _():
            take_y(k - 1, CHUNK)

        @pl.when(k >= 2)
        def _():
            take_s(k - 2, CHUNK)

        @pl.when(k + AHEAD < full)
        def _():
            open_chunk(k + AHEAD, CHUNK)

        if last:

            @pl.when(k + AHEAD == full)
            def _():
                open_chunk(full, last)

    def loads(f, rows):
        slot = f % 2
        r = rows_of(f, rows)
        sources = [w_ref.at[r]] + [wbuf.at[b, r] for b in order[1:]]
        return [
            pltpu.make_async_copy(src, wv.at[slot, j, pl.ds(0, rows)], ld_sem.at[slot, j])
            for j, src in enumerate(sources)
        ]

    def tile(f, rows, next_rows):
        for copy in loads(f, rows):
            copy.wait()
        if next_rows:
            for copy in loads(f + 1, next_rows):
                copy.start()
        slot = f % 2
        r = rows_of(f, rows)
        grad = None
        for j, b in enumerate(order):
            term = lax.dot_general(
                gbuf[b],
                wv[slot, j, pl.ds(0, rows), :],
                (((1,), (1,)), ((), ())),
                preferred_element_type=jnp.float32,
            )
            grad = term if grad is None else grad + term
        gate_value = gate_v[:, r].astype(jnp.float32)
        up_value = up_v[:, r].astype(jnp.float32)
        sig = 1.0 / (1.0 + jnp.exp(-gate_value))
        hidden = (gate_value * sig * up_value).astype(jnp.bfloat16)
        grad_up = (grad * gate_value * sig).astype(jnp.bfloat16)
        grad_gate = (grad * up_value * sig * (1.0 + gate_value * (1.0 - sig))).astype(jnp.bfloat16)
        proj_ref[0] += contract_cols(grad_gate, og_ref[:, r])
        proj_ref[1] += contract_cols(grad_up, ou_ref[:, r])
        proj_ref[2] += contract_cols(hidden, id_ref[:, r])

    def tiles(lo, hi):
        @pl.loop(lo, hi)
        def _(f):
            tile(f, CHUNK, CHUNK)

    @pl.loop(0, z_steps)
    def _(k):
        z_duty(k)
        traffic(k)

    own_gate.wait()
    own_up.wait()
    for copy in loads(0, CHUNK):
        copy.start()

    done = 3
    tiles(0, done)
    for k in range(z_steps, full):
        traffic(k)
        ready = k - 2
        step = min(ready, done + 4)
        tiles(done, step)
        done = step
    if last:
        take_x(full, last)
    take_y(full - 1, CHUNK)
    take_s(full - 2, CHUNK)
    tiles(done, full - 2)
    if last:
        take_y(full, last)
    take_s(full - 1, CHUNK)
    tiles(full - 2, full - 1)
    if last:
        take_s(full, last)
    tile(full - 1, CHUNK, last)
    if last:
        tile(full, last, 0)

    def drain(k, rows):
        x_copy(k, rows).wait_send()
        y_copy(k, rows).wait_send()
        s0_copy(k, rows, d).wait_send()
        s_copy(1, k, rows, far).wait_send()
        s_copy(2, k, rows, far).wait_send()

    @pl.loop(0, full)
    def _(k):
        drain(k, CHUNK)

    if last:
        drain(full, last)

    @pl.loop(0, z_steps)
    def _(n):
        @pl.when((z > 0) & (n < PIECES * (blocks - z)))
        def _():
            dn_copy(n, z).wait_send()

        @pl.when((z < blocks - 1) & (n < PIECES * (z + 1)))
        def _():
            up_copy(n, z).wait_send()


def backprop(down_weight, out_grad, gate_pre, up_pre, out_gate, out_up, in_down, blocks):
    hidden_rows, depth = down_weight.shape
    tokens = out_grad.shape[0]
    rank = out_gate.shape[1]
    chunks = pl.cdiv(hidden_rows, CHUNK)
    z_steps = PIECES * (blocks - 1)
    anywhere = pl.BlockSpec(memory_space=pl.ANY)
    local = pl.BlockSpec(memory_space=pltpu.VMEM)
    dma = pltpu.SemaphoreType.DMA
    proj, _ = pl.pallas_call(
        backprop_kernel,
        out_shape=(
            jax.ShapeDtypeStruct((3, tokens, rank), jnp.float32),
            jax.ShapeDtypeStruct((blocks, hidden_rows, depth), jnp.bfloat16),
        ),
        in_specs=[anywhere] * 4 + [local] * 3,
        out_specs=(local, anywhere),
        scratch_shapes=[
            pltpu.VMEM((blocks, tokens, depth), jnp.bfloat16),
            pltpu.VMEM(gate_pre.shape, jnp.bfloat16),
            pltpu.VMEM(up_pre.shape, jnp.bfloat16),
            pltpu.VMEM((2, blocks, CHUNK, depth), jnp.bfloat16),
            dma((3,)),
            dma((2, blocks)),
            dma((chunks,)),
            dma((chunks,)),
            dma((chunks,)),
            dma((chunks,)),
            dma((3, chunks)),
            dma((3, chunks)),
            dma((z_steps,)),
            dma((z_steps,)),
            dma((z_steps,)),
            dma((z_steps,)),
        ],
        compiler_params=pltpu.CompilerParams(
            collective_id=0, has_side_effects=True, vmem_limit_bytes=50 * 2**20
        ),
        cost_estimate=pl.CostEstimate(
            flops=2 * tokens * hidden_rows * depth * blocks,
            bytes_accessed=2 * blocks * hidden_rows * depth * 2,
            transcendentals=tokens * hidden_rows,
        ),
    )(down_weight, out_grad, gate_pre, up_pre, out_gate.T, out_up.T, in_down.T)
    return proj


def sketch_kernel(proj_ref, weight_ref, out_ref, rows_buf, sketch_buf, r_send, r_recv, k_send, k_recv):
    parts = rows_buf.shape[0]
    share = rows_buf.shape[1]
    rank = sketch_buf.shape[2]
    z = lax.axis_index("tensor")
    barrier = pltpu.get_barrier_semaphore()
    peers = [lax.rem(z + step, parts) for step in range(1, parts)]
    for peer in peers:
        pl.semaphore_signal(barrier, inc=1, device_id={"tensor": peer}, device_id_type=MESH)
    pl.semaphore_wait(barrier, parts - 1)

    def share_of(owner):
        return pl.ds(pl.multiple_of(owner * share, share), share)

    def rows_copy(i):
        return pltpu.make_async_remote_copy(
            src_ref=proj_ref.at[share_of(peers[i])],
            dst_ref=rows_buf.at[z],
            send_sem=r_send.at[i],
            recv_sem=r_recv.at[i],
            device_id={"tensor": peers[i]},
            device_id_type=MESH,
        )

    def sketch_copy(i):
        return pltpu.make_async_remote_copy(
            src_ref=sketch_buf.at[z],
            dst_ref=sketch_buf.at[z],
            send_sem=k_send.at[i],
            recv_sem=k_recv.at[i],
            device_id={"tensor": peers[i]},
            device_id_type=MESH,
        )

    for i in range(parts - 1):
        rows_copy(i).start()
    rows_buf[z] = proj_ref[share_of(z), :]
    for i in range(parts - 1):
        rows_copy(i).wait()
    total = rows_buf[0]
    for i in range(1, parts):
        total = total + rows_buf[i]
    scaled = total * weight_ref[share_of(z), :]
    width = 2 * rank
    products = []
    for layer in range(3):
        cols = slice(layer * width, (layer + 1) * width)
        products.append(
            lax.dot_general(
                scaled[:, cols],
                total[:, cols],
                (((0,), (0,)), ((), ())),
                precision=lax.Precision.HIGHEST,
                preferred_element_type=jnp.float32,
            )
        )
    lane = lax.broadcasted_iota(jnp.int32, (rank, width), 1)
    sketch_buf[z, 0] = jnp.where(
        lane < rank, products[1][rank:, :], products[0][:rank, :]
    )
    sketch_buf[z, 1] = products[2][:rank, :]
    for i in range(parts - 1):
        sketch_copy(i).start()
    for i in range(parts - 1):
        sketch_copy(i).wait()
    examples = out_ref.shape[0]
    each = parts // examples
    for e in range(examples):
        result = sketch_buf[e * each]
        for i in range(1, each):
            result = result + sketch_buf[e * each + i]
        out_ref[e] = result


def sketch_sums(proj, weights, parts):
    tokens, width = proj.shape
    examples = weights.shape[0]
    rank = width // 6
    share = tokens // parts
    local = pl.BlockSpec(memory_space=pltpu.VMEM)
    dma = pltpu.SemaphoreType.DMA
    packed = pl.pallas_call(
        sketch_kernel,
        out_shape=jax.ShapeDtypeStruct((examples, 2, rank, 2 * rank), jnp.float32),
        in_specs=[local, local],
        out_specs=local,
        scratch_shapes=[
            pltpu.VMEM((parts, share, width), jnp.float32),
            pltpu.VMEM((parts, 2, rank, 2 * rank), jnp.float32),
            dma((parts - 1,)),
            dma((parts - 1,)),
            dma((parts - 1,)),
            dma((parts - 1,)),
        ],
        compiler_params=pltpu.CompilerParams(
            collective_id=1, has_side_effects=True, vmem_limit_bytes=24 * 2**20
        ),
    )(proj, jnp.sum(weights, axis=0)[:, None])
    layers = [packed[:, 0, :, rank:], packed[:, 0, :, :rank], packed[:, 1, :, rank:]]
    return jnp.stack(layers, axis=1).reshape(examples, 3, rank * rank)


def gathered(out_grad, gate_pre, up_pre, down_weight, out_gate, out_up, in_down):
    full_grad = lax.all_gather(out_grad, "tensor", axis=1, tiled=True)
    grad_hidden = contract_cols(full_grad, lax.all_gather(down_weight, "dp", axis=1, tiled=True))
    gate_value = gate_pre.astype(jnp.float32)
    up_value = up_pre.astype(jnp.float32)
    sigmoid_gate = jax.nn.sigmoid(gate_value)
    hidden = (gate_value * sigmoid_gate * up_value).astype(jnp.bfloat16)
    grad_up = (grad_hidden * gate_value * sigmoid_gate).astype(jnp.bfloat16)
    grad_gate = (
        grad_hidden * up_value * sigmoid_gate * (1.0 + gate_value * (1.0 - sigmoid_gate))
    ).astype(jnp.bfloat16)
    return (
        jnp.dot(grad_gate, out_gate, preferred_element_type=jnp.float32),
        jnp.dot(grad_up, out_up, preferred_element_type=jnp.float32),
        jnp.dot(hidden, in_down, preferred_element_type=jnp.float32),
    )


def shards(
    fused,
    inputs,
    out_grad,
    gate_pre,
    up_pre,
    down_weight,
    in_gate,
    out_gate,
    in_up,
    out_up,
    in_down,
    out_down,
    counts,
    query_ids,
):
    tok_rows = inputs.shape[0]
    if fused:
        grads = backprop(
            down_weight, out_grad, gate_pre, up_pre, out_gate, out_up, in_down, lax.axis_size("tensor")
        )
    else:
        grads = gathered(out_grad, gate_pre, up_pre, down_weight, out_gate, out_up, in_down)
    in_proj = [
        jnp.dot(inputs, in_gate, preferred_element_type=jnp.float32),
        jnp.dot(inputs, in_up, preferred_element_type=jnp.float32),
        jnp.dot(out_grad, out_down, preferred_element_type=jnp.float32),
    ]
    weights = token_weights(jnp.arange(tok_rows, dtype=jnp.int32), counts)
    if fused:
        columns = [in_proj[0], grads[0], grads[1], in_proj[1], grads[2], in_proj[2]]
        sketches = sketch_sums(jnp.concatenate(columns, axis=1), weights, lax.axis_size("tensor"))
    else:
        columns = [in_proj[0], grads[0], in_proj[1], grads[1], grads[2], in_proj[2]]
        proj = lax.psum(jnp.concatenate(columns, axis=1), "tensor")
        sketches = outer_sums(proj, weights)
    every_sketch = lax.all_gather(sketches.astype(jnp.bfloat16), "dp", axis=0, tiled=True).astype(
        sketches.dtype
    )
    owners = jnp.arange(every_sketch.shape[0], dtype=jnp.int32)
    select = (query_ids[:, None] == owners[None, :]).astype(jnp.float32)
    query = jnp.einsum("qe,elf->qlf", select, every_sketch, precision=lax.Precision.HIGHEST)
    return (sketches, cosines(sketches, query))


def solution(mesh):
    sizes = dict(mesh.shape)
    fused = sizes["parts"] == 2 and sizes["dp"] == 4 and sizes["tensor"] == 4
    return jax.shard_map(
        functools.partial(shards, fused),
        mesh=mesh,
        in_specs=(
            P(("parts", "dp"), "tensor"),
            P(("parts", "dp"), "tensor"),
            P(("parts", "dp"), "tensor"),
            P(("parts", "dp"), "tensor"),
            P("tensor", "dp"),
            P("tensor", None),
            P("tensor", None),
            P("tensor", None),
            P("tensor", None),
            P("tensor", None),
            P("tensor", None),
            P(("parts", "dp")),
            P("parts"),
        ),
        out_specs=(P(("parts", "dp"), None, None), P(("parts", "dp"), None)),
        check_vma=False,
    )
```

```python
import functools
import math

import jax
import jax.numpy as jnp
from jax import lax
from jax.experimental import pallas as pl
from jax.experimental.pallas import tpu as pltpu
from jax.sharding import PartitionSpec as P

SEQ = 224


def token_weights(rows, counts):
    slot = rows // SEQ
    place = rows % SEQ
    owners = jnp.arange(counts.shape[0], dtype=jnp.int32)
    hit = (slot[None, :] == owners[:, None]) & (place[None, :] < counts[:, None])
    return hit.astype(jnp.float32) * (1.0 / math.sqrt(SEQ))


def outer_sums(proj, weights):
    shaped = proj.reshape(proj.shape[0], 3, 2, -1)
    result = jnp.einsum(
        "en,nli,nlj->elij",
        weights,
        shaped[:, :, 0, :],
        shaped[:, :, 1, :],
        precision=lax.Precision.HIGHEST,
    )
    return result.reshape(result.shape[0], 3, -1)


def cosines(sketches, query):
    left = sketches.reshape(sketches.shape[0], -1)
    right = query.reshape(query.shape[0], -1)
    inner = jnp.einsum("ef,qf->eq", left, right, precision=lax.Precision.HIGHEST)
    left_norm = jnp.sqrt(jnp.sum(left * left, axis=1) + 1e-06)
    right_norm = jnp.sqrt(jnp.sum(right * right, axis=1) + 1e-06)
    return inner / (left_norm[:, None] * right_norm[None, :])


def contract_cols(left, right):
    return lax.dot_general(
        left, right, (((1,), (1,)), ((), ())), preferred_element_type=jnp.float32
    )


CHUNK = 256
AHEAD = 4
PIECES = 4
MESH = pl.DeviceIdType.MESH


def backprop_kernel(
    w_ref,
    g_ref,
    gate_ref,
    up_ref,
    og_ref,
    ou_ref,
    id_ref,
    proj_ref,
    wbuf,
    gbuf,
    gate_v,
    up_v,
    wv,
    own_sem,
    ld_sem,
    x_send,
    x_recv,
    y_send,
    y_recv,
    s_send,
    s_recv,
    dn_send,
    dn_recv,
    up_send,
    up_recv,
):
    hidden_rows, depth = w_ref.shape
    tokens = g_ref.shape[0]
    blocks = gbuf.shape[0]
    half = depth // 2
    full = hidden_rows // CHUNK
    last = hidden_rows - full * CHUNK
    piece = tokens // PIECES
    z_steps = PIECES * (blocks - 1)

    y = lax.axis_index("parts")
    z = lax.axis_index("tensor")
    d = lax.axis_index("dp")
    sib = d + 1 - 2 * (d % 2)
    far = (d + 2) % 4
    far_sib = far + 1 - 2 * (far % 2)
    order = (d, sib, far, far_sib)

    def rows_of(k, rows):
        return pl.ds(pl.multiple_of(k * CHUNK, CHUNK), rows)

    def cols_of(h):
        return pl.ds(pl.multiple_of(h * half, half), half)

    def remote(src, dst, send, recv, device):
        return pltpu.make_async_remote_copy(
            src_ref=src,
            dst_ref=dst,
            send_sem=send,
            recv_sem=recv,
            device_id=device,
            device_id_type=MESH,
        )

    def x_copy(k, rows):
        r = rows_of(k, rows)
        return remote(
            w_ref.at[r, cols_of(y)],
            wbuf.at[d, r, cols_of(y)],
            x_send.at[k],
            x_recv.at[k],
            {"dp": far},
        )

    def x_arrival(k, rows):
        r = rows_of(k, rows)
        return remote(
            w_ref.at[r, cols_of(y)],
            wbuf.at[far, r, cols_of(y)],
            x_send.at[k],
            x_recv.at[k],
            {"dp": far},
        )

    def y_copy(k, rows):
        r = rows_of(k, rows)
        block = wbuf.at[far, r, cols_of(y)]
        return remote(block, block, y_send.at[k], y_recv.at[k], {"parts": 1 - y})

    def y_arrival(k, rows):
        r = rows_of(k, rows)
        block = wbuf.at[far, r, cols_of(1 - y)]
        return remote(block, block, y_send.at[k], y_recv.at[k], {"parts": 1 - y})

    def s0_copy(k, rows, block):
        r = rows_of(k, rows)
        return remote(
            w_ref.at[r], wbuf.at[block, r], s_send.at[0, k], s_recv.at[0, k], {"dp": sib}
        )

    def s_copy(kind, k, rows, block):
        r = rows_of(k, rows)
        h = y if kind == 1 else 1 - y
        view = wbuf.at[block, r, cols_of(h)]
        return remote(view, view, s_send.at[kind, k], s_recv.at[kind, k], {"dp": sib})

    def z_rows(n):
        return pl.ds(pl.multiple_of((n % PIECES) * piece, piece), piece)

    def dn_copy(n, first):
        view = gbuf.at[first + n // PIECES, z_rows(n)]
        return remote(view, view, dn_send.at[n], dn_recv.at[n], {"tensor": z - 1})

    def up_copy(n, first):
        view = gbuf.at[first - n // PIECES, z_rows(n)]
        return remote(view, view, up_send.at[n], up_recv.at[n], {"tensor": z + 1})

    def z_duty(n):
        @pl.when(n < PIECES * (blocks - 1 - z))
        def _():
            dn_copy(n, z + 1).wait_recv()

            @pl.when(z > 0)
            def _():
                dn_copy(n + PIECES, z).start()

        @pl.when(n < PIECES * z)
        def _():
            up_copy(n, z - 1).wait_recv()

            @pl.when(z < blocks - 1)
            def _():
                up_copy(n + PIECES, z).start()

    own_g = pltpu.make_async_copy(g_ref, gbuf.at[z], own_sem.at[0])
    own_gate = pltpu.make_async_copy(gate_ref, gate_v, own_sem.at[1])
    own_up = pltpu.make_async_copy(up_ref, up_v, own_sem.at[2])
    own_g.start()

    barrier = pltpu.get_barrier_semaphore()
    for device in ({"dp": sib}, {"dp": far}, {"parts": 1 - y}):
        pl.semaphore_signal(barrier, inc=1, device_id=device, device_id_type=MESH)

    @pl.when(z > 0)
    def _():
        pl.semaphore_signal(barrier, inc=1, device_id={"tensor": z - 1}, device_id_type=MESH)

    @pl.when(z < blocks - 1)
    def _():
        pl.semaphore_signal(barrier, inc=1, device_id={"tensor": z + 1}, device_id_type=MESH)

    neighbours = 3 + (z > 0).astype(jnp.int32) + (z < blocks - 1).astype(jnp.int32)
    pl.semaphore_wait(barrier, neighbours)

    def open_chunk(k, rows):
        x_copy(k, rows).start()
        s0_copy(k, rows, d).start()

    for k in range(AHEAD):
        open_chunk(k, CHUNK)
    own_g.wait()

    @pl.when(z > 0)
    def _():
        for n in range(PIECES):
            dn_copy(n, z).start()

    @pl.when(z < blocks - 1)
    def _():
        for n in range(PIECES):
            up_copy(n, z).start()

    own_gate.start()
    own_up.start()
    proj_ref[...] = jnp.zeros_like(proj_ref)

    def take_x(k, rows):
        x_arrival(k, rows).wait_recv()
        y_copy(k, rows).start()
        s_copy(1, k, rows, far).start()
        s0_copy(k, rows, sib).wait_recv()

    def take_y(k, rows):
        y_arrival(k, rows).wait_recv()
        s_copy(2, k, rows, far).start()
        s_copy(1, k, rows, far_sib).wait_recv()

    def take_s(k, rows):
        s_copy(2, k, rows, far_sib).wait_recv()

    def traffic(k):
        take_x(k, CHUNK)

        @pl.when(k >= 1)
        def _():
            take_y(k - 1, CHUNK)

        @pl.when(k >= 2)
        def _():
            take_s(k - 2, CHUNK)

        @pl.when(k + AHEAD < full)
        def _():
            open_chunk(k + AHEAD, CHUNK)

        if last:

            @pl.when(k + AHEAD == full)
            def _():
                open_chunk(full, last)

    def loads(f, rows):
        slot = f % 2
        r = rows_of(f, rows)
        sources = [w_ref.at[r]] + [wbuf.at[b, r] for b in order[1:]]
        return [
            pltpu.make_async_copy(src, wv.at[slot, j, pl.ds(0, rows)], ld_sem.at[slot, j])
            for j, src in enumerate(sources)
        ]

    def tile(f, rows, next_rows):
        for copy in loads(f, rows):
            copy.wait()
        if next_rows:
            for copy in loads(f + 1, next_rows):
                copy.start()
        slot = f % 2
        r = rows_of(f, rows)
        grad = None
        for j, b in enumerate(order):
            term = lax.dot_general(
                gbuf[b],
                wv[slot, j, pl.ds(0, rows), :],
                (((1,), (1,)), ((), ())),
                preferred_element_type=jnp.float32,
            )
            grad = term if grad is None else grad + term
        gate_value = gate_v[:, r].astype(jnp.float32)
        up_value = up_v[:, r].astype(jnp.float32)
        sig = 1.0 / (1.0 + jnp.exp(-gate_value))
        hidden = (gate_value * sig * up_value).astype(jnp.bfloat16)
        grad_up = (grad * gate_value * sig).astype(jnp.bfloat16)
        grad_gate = (grad * up_value * sig * (1.0 + gate_value * (1.0 - sig))).astype(jnp.bfloat16)
        proj_ref[0] += contract_cols(grad_gate, og_ref[:, r])
        proj_ref[1] += contract_cols(grad_up, ou_ref[:, r])
        proj_ref[2] += contract_cols(hidden, id_ref[:, r])

    def tiles(lo, hi):
        @pl.loop(lo, hi)
        def _(f):
            tile(f, CHUNK, CHUNK)

    @pl.loop(0, z_steps)
    def _(k):
        z_duty(k)
        traffic(k)

    own_gate.wait()
    own_up.wait()
    for copy in loads(0, CHUNK):
        copy.start()

    done = 4
    tiles(0, done)
    for k in range(z_steps, full):
        traffic(k)
        ready = k - 2
        step = min(ready, done + 4)
        tiles(done, step)
        done = step
    if last:
        take_x(full, last)
    take_y(full - 1, CHUNK)
    take_s(full - 2, CHUNK)
    tiles(done, full - 2)
    if last:
        take_y(full, last)
    take_s(full - 1, CHUNK)
    tiles(full - 2, full - 1)
    if last:
        take_s(full, last)
    tile(full - 1, CHUNK, last)
    if last:
        tile(full, last, 0)

    def drain(k, rows):
        x_copy(k, rows).wait_send()
        y_copy(k, rows).wait_send()
        s0_copy(k, rows, d).wait_send()
        s_copy(1, k, rows, far).wait_send()
        s_copy(2, k, rows, far).wait_send()

    @pl.loop(0, full)
    def _(k):
        drain(k, CHUNK)

    if last:
        drain(full, last)

    @pl.loop(0, z_steps)
    def _(n):
        @pl.when((z > 0) & (n < PIECES * (blocks - z)))
        def _():
            dn_copy(n, z).wait_send()

        @pl.when((z < blocks - 1) & (n < PIECES * (z + 1)))
        def _():
            up_copy(n, z).wait_send()


def backprop(down_weight, out_grad, gate_pre, up_pre, out_gate, out_up, in_down, blocks):
    hidden_rows, depth = down_weight.shape
    tokens = out_grad.shape[0]
    rank = out_gate.shape[1]
    chunks = pl.cdiv(hidden_rows, CHUNK)
    z_steps = PIECES * (blocks - 1)
    anywhere = pl.BlockSpec(memory_space=pl.ANY)
    local = pl.BlockSpec(memory_space=pltpu.VMEM)
    dma = pltpu.SemaphoreType.DMA
    proj, _ = pl.pallas_call(
        backprop_kernel,
        out_shape=(
            jax.ShapeDtypeStruct((3, tokens, rank), jnp.float32),
            jax.ShapeDtypeStruct((blocks, hidden_rows, depth), jnp.bfloat16),
        ),
        in_specs=[anywhere] * 4 + [local] * 3,
        out_specs=(local, anywhere),
        scratch_shapes=[
            pltpu.VMEM((blocks, tokens, depth), jnp.bfloat16),
            pltpu.VMEM(gate_pre.shape, jnp.bfloat16),
            pltpu.VMEM(up_pre.shape, jnp.bfloat16),
            pltpu.VMEM((2, blocks, CHUNK, depth), jnp.bfloat16),
            dma((3,)),
            dma((2, blocks)),
            dma((chunks,)),
            dma((chunks,)),
            dma((chunks,)),
            dma((chunks,)),
            dma((3, chunks)),
            dma((3, chunks)),
            dma((z_steps,)),
            dma((z_steps,)),
            dma((z_steps,)),
            dma((z_steps,)),
        ],
        compiler_params=pltpu.CompilerParams(
            collective_id=0, has_side_effects=True, vmem_limit_bytes=50 * 2**20
        ),
        cost_estimate=pl.CostEstimate(
            flops=2 * tokens * hidden_rows * depth * blocks,
            bytes_accessed=2 * blocks * hidden_rows * depth * 2,
            transcendentals=tokens * hidden_rows,
        ),
    )(down_weight, out_grad, gate_pre, up_pre, out_gate.T, out_up.T, in_down.T)
    return proj


def sketch_kernel(proj_ref, weight_ref, out_ref, rows_buf, sketch_buf, r_send, r_recv, k_send, k_recv):
    parts = rows_buf.shape[0]
    share = rows_buf.shape[1]
    rank = sketch_buf.shape[2]
    z = lax.axis_index("tensor")
    barrier = pltpu.get_barrier_semaphore()
    peers = [lax.rem(z + step, parts) for step in range(1, parts)]
    for peer in peers:
        pl.semaphore_signal(barrier, inc=1, device_id={"tensor": peer}, device_id_type=MESH)
    pl.semaphore_wait(barrier, parts - 1)

    def share_of(owner):
        return pl.ds(pl.multiple_of(owner * share, share), share)

    def rows_copy(i):
        return pltpu.make_async_remote_copy(
            src_ref=proj_ref.at[share_of(peers[i])],
            dst_ref=rows_buf.at[z],
            send_sem=r_send.at[i],
            recv_sem=r_recv.at[i],
            device_id={"tensor": peers[i]},
            device_id_type=MESH,
        )

    def sketch_copy(i):
        return pltpu.make_async_remote_copy(
            src_ref=sketch_buf.at[z],
            dst_ref=sketch_buf.at[z],
            send_sem=k_send.at[i],
            recv_sem=k_recv.at[i],
            device_id={"tensor": peers[i]},
            device_id_type=MESH,
        )

    for i in range(parts - 1):
        rows_copy(i).start()
    rows_buf[z] = proj_ref[share_of(z), :]
    for i in range(parts - 1):
        rows_copy(i).wait()
    total = rows_buf[0]
    for i in range(1, parts):
        total = total + rows_buf[i]
    scaled = total * weight_ref[share_of(z), :]
    width = 2 * rank
    products = []
    for layer in range(3):
        cols = slice(layer * width, (layer + 1) * width)
        products.append(
            lax.dot_general(
                scaled[:, cols],
                total[:, cols],
                (((0,), (0,)), ((), ())),
                precision=lax.Precision.HIGHEST,
                preferred_element_type=jnp.float32,
            )
        )
    lane = lax.broadcasted_iota(jnp.int32, (rank, width), 1)
    sketch_buf[z, 0] = jnp.where(
        lane < rank, products[1][rank:, :], products[0][:rank, :]
    )
    sketch_buf[z, 1] = products[2][:rank, :]
    for i in range(parts - 1):
        sketch_copy(i).start()
    for i in range(parts - 1):
        sketch_copy(i).wait()
    examples = out_ref.shape[0]
    each = parts // examples
    for e in range(examples):
        result = sketch_buf[e * each]
        for i in range(1, each):
            result = result + sketch_buf[e * each + i]
        out_ref[e] = result


def sketch_sums(proj, weights, parts):
    tokens, width = proj.shape
    examples = weights.shape[0]
    rank = width // 6
    share = tokens // parts
    local = pl.BlockSpec(memory_space=pltpu.VMEM)
    dma = pltpu.SemaphoreType.DMA
    packed = pl.pallas_call(
        sketch_kernel,
        out_shape=jax.ShapeDtypeStruct((examples, 2, rank, 2 * rank), jnp.float32),
        in_specs=[local, local],
        out_specs=local,
        scratch_shapes=[
            pltpu.VMEM((parts, share, width), jnp.float32),
            pltpu.VMEM((parts, 2, rank, 2 * rank), jnp.float32),
            dma((parts - 1,)),
            dma((parts - 1,)),
            dma((parts - 1,)),
            dma((parts - 1,)),
        ],
        compiler_params=pltpu.CompilerParams(
            collective_id=1, has_side_effects=True, vmem_limit_bytes=24 * 2**20
        ),
    )(proj, jnp.sum(weights, axis=0)[:, None])
    layers = [packed[:, 0, :, rank:], packed[:, 0, :, :rank], packed[:, 1, :, rank:]]
    return jnp.stack(layers, axis=1).reshape(examples, 3, rank * rank)


def gathered(out_grad, gate_pre, up_pre, down_weight, out_gate, out_up, in_down):
    full_grad = lax.all_gather(out_grad, "tensor", axis=1, tiled=True)
    grad_hidden = contract_cols(full_grad, lax.all_gather(down_weight, "dp", axis=1, tiled=True))
    gate_value = gate_pre.astype(jnp.float32)
    up_value = up_pre.astype(jnp.float32)
    sigmoid_gate = jax.nn.sigmoid(gate_value)
    hidden = (gate_value * sigmoid_gate * up_value).astype(jnp.bfloat16)
    grad_up = (grad_hidden * gate_value * sigmoid_gate).astype(jnp.bfloat16)
    grad_gate = (
        grad_hidden * up_value * sigmoid_gate * (1.0 + gate_value * (1.0 - sigmoid_gate))
    ).astype(jnp.bfloat16)
    return (
        jnp.dot(grad_gate, out_gate, preferred_element_type=jnp.float32),
        jnp.dot(grad_up, out_up, preferred_element_type=jnp.float32),
        jnp.dot(hidden, in_down, preferred_element_type=jnp.float32),
    )


def shards(
    fused,
    inputs,
    out_grad,
    gate_pre,
    up_pre,
    down_weight,
    in_gate,
    out_gate,
    in_up,
    out_up,
    in_down,
    out_down,
    counts,
    query_ids,
):
    tok_rows = inputs.shape[0]
    if fused:
        grads = backprop(
            down_weight, out_grad, gate_pre, up_pre, out_gate, out_up, in_down, lax.axis_size("tensor")
        )
    else:
        grads = gathered(out_grad, gate_pre, up_pre, down_weight, out_gate, out_up, in_down)
    in_proj = [
        jnp.dot(inputs, in_gate, preferred_element_type=jnp.float32),
        jnp.dot(inputs, in_up, preferred_element_type=jnp.float32),
        jnp.dot(out_grad, out_down, preferred_element_type=jnp.float32),
    ]
    weights = token_weights(jnp.arange(tok_rows, dtype=jnp.int32), counts)
    if fused:
        columns = [in_proj[0], grads[0], grads[1], in_proj[1], grads[2], in_proj[2]]
        sketches = sketch_sums(jnp.concatenate(columns, axis=1), weights, lax.axis_size("tensor"))
    else:
        columns = [in_proj[0], grads[0], in_proj[1], grads[1], grads[2], in_proj[2]]
        proj = lax.psum(jnp.concatenate(columns, axis=1), "tensor")
        sketches = outer_sums(proj, weights)
    every_sketch = lax.all_gather(sketches.astype(jnp.bfloat16), "dp", axis=0, tiled=True).astype(
        sketches.dtype
    )
    owners = jnp.arange(every_sketch.shape[0], dtype=jnp.int32)
    select = (query_ids[:, None] == owners[None, :]).astype(jnp.float32)
    query = jnp.einsum("qe,elf->qlf", select, every_sketch, precision=lax.Precision.HIGHEST)
    return (sketches, cosines(sketches, query))


def solution(mesh):
    sizes = dict(mesh.shape)
    fused = sizes["parts"] == 2 and sizes["dp"] == 4 and sizes["tensor"] == 4
    return jax.shard_map(
        functools.partial(shards, fused),
        mesh=mesh,
        in_specs=(
            P(("parts", "dp"), "tensor"),
            P(("parts", "dp"), "tensor"),
            P(("parts", "dp"), "tensor"),
            P(("parts", "dp"), "tensor"),
            P("tensor", "dp"),
            P("tensor", None),
            P("tensor", None),
            P("tensor", None),
            P("tensor", None),
            P("tensor", None),
            P("tensor", None),
            P(("parts", "dp")),
            P("parts"),
        ),
        out_specs=(P(("parts", "dp"), None, None), P(("parts", "dp"), None)),
        check_vma=False,
    )
```
